128 devices in a mesh: wide: 16 (over x, y), narrow: 8 (over z, core).
Axes of the slice: x: 4, y: 4, z: 4, core: 2. Of those that a mesh axis runs over, the one named last changes fastest.
Arguments:
- query_proj: bfloat16 [32768, 2048], P(('wide', 'narrow')), may hold values from -20 to 20
- key_proj: bfloat16 [32768, 2048], P(('wide', 'narrow')), may hold values from -20 to 20
- value_proj: bfloat16 [32768, 2048], P(('wide', 'narrow')), may hold values from -6 to 6
- positions: int32 [3, 32768], P(None, ('wide', 'narrow')), may hold values from 0 to 142, as said below
- key_lists: int32 [256, 24], replicated, may hold values from 0 to 255, as said below
- key_counts: int32 [256], replicated, may hold values from 6 to 24
Outputs:
- attended: bfloat16 [32768, 2048], P(('wide', 'narrow'))
The draws below stay inside these ranges and needn't reach their ends.
Inputs may be any that keep to these rules, and one draw needn't show every extreme that they name: `key_lists`: each list holds distinct key blocks and always its own query block; entries after the first key_counts ones repeat the own block. Over the query blocks of one frame of 16 blocks, at most 4 distinct blocks of any other frame are listed, and exactly 4 of each adjacent frame; a query block may list no block of some farther frames. `positions`: Rows: frame id, height id, width id.
All inputs are finite; a program needn't handle non-finite values.
Results may differ from the reference program's by a relative error of at most 0.012.
Values may be sent and summed in bfloat16 or wider, within the bound.
No kernel may reach another device: no remote copies, remote signals or barrier semaphores. Data moves between devices by JAX's collectives and lax.ppermute only.
A program may use at most 128 MiB of HBM per device.

```python
import jax
import jax.numpy as jnp
from jax import lax

HEADS = 16
HD = 128
BLOCK = 128
CAP = 4
FRAME = 2048
FBLOCKS = 16
TOKENS = 32768
QBLOCKS = 256
KMAX = 24
N_WIDE = 16


def draw_query_proj(key, part):
    key = jax.random.fold_in(key, 1)
    values = jnp.clip(jax.random.normal(key, (TOKENS, HEADS, HD), jnp.float32), -6.0, 6.0)
    return values.reshape(TOKENS, HEADS * HD).astype(jnp.bfloat16)


def draw_key_proj(key, part):
    key = jax.random.fold_in(key, 2)
    values = jnp.clip(jax.random.normal(key, (TOKENS, HEADS, HD), jnp.float32), -6.0, 6.0)
    return values.reshape(TOKENS, HEADS * HD).astype(jnp.bfloat16)


def draw_positions(key, part):
    key = jax.random.fold_in(key, 3)
    key_frame, key_height, key_width = jax.random.split(key, 3)
    token_ids = jnp.arange(TOKENS, dtype=jnp.int32)
    frame_ids = token_ids // FRAME
    inner = token_ids % FRAME
    frame_shift = jax.random.randint(key_frame, (), 0, 8)
    height_shift = jax.random.randint(key_height, (N_WIDE,), 0, 16)
    height_shift = height_shift.at[0].set(0).at[N_WIDE - 1].set(15)
    width_shift = jax.random.randint(key_width, (N_WIDE,), 0, 16)
    width_shift = width_shift.at[0].set(0).at[N_WIDE - 1].set(15)
    frame_row = frame_ids + frame_shift
    height_row = inner // BLOCK + height_shift[frame_ids]
    width_row = inner % BLOCK + width_shift[frame_ids]
    return jnp.stack([frame_row, height_row, width_row], axis=0).astype(jnp.int32)


def block_lists(key):
    key = jax.random.fold_in(key, 7)
    key_anchor, key_pick, key_far = jax.random.split(key, 3)
    ranks = jax.random.randint(key_anchor, (N_WIDE, N_WIDE, FBLOCKS), 0, 2 ** 20) * FBLOCKS
    ranks = ranks + jnp.arange(FBLOCKS, dtype=jnp.int32)
    anchors = jnp.argsort(ranks, axis=-1, stable=True)[..., :CAP].astype(jnp.int32)
    picked = jax.random.randint(key_pick, (QBLOCKS, N_WIDE), 0, CAP)
    far_keep = jax.random.randint(key_far, (QBLOCKS, N_WIDE), 0, 4) > 0
    far_keep = far_keep.at[FBLOCKS + 1].set(True)
    row_ids = jnp.arange(QBLOCKS, dtype=jnp.int32)
    frame_ids = row_ids // FBLOCKS
    inner = row_ids % FBLOCKS
    steps_own = jnp.array([-1, 0, 1], dtype=jnp.int32)
    own_ids = frame_ids[:, None] * FBLOCKS + inner[:, None] + steps_own[None, :]
    own_live = (inner[:, None] + steps_own[None, :] >= 0) & (inner[:, None] + steps_own[None, :] < FBLOCKS)
    row_anchors = anchors[frame_ids]
    distance = jnp.abs(jnp.arange(N_WIDE, dtype=jnp.int32)[None, :] - frame_ids[:, None])
    chosen = jnp.take_along_axis(row_anchors, picked[:, :, None], axis=2)
    slot_ids = jnp.arange(CAP, dtype=jnp.int32)[None, None, :]
    far_block = ((distance >= 2) & far_keep)[:, :, None] & (slot_ids == 0)
    remote_pos = jnp.where(far_block, chosen, row_anchors)
    remote_ids = jnp.arange(N_WIDE, dtype=jnp.int32)[None, :, None] * FBLOCKS + remote_pos
    remote_live = (distance == 1)[:, :, None] | far_block
    all_ids = jnp.concatenate([own_ids, remote_ids.reshape(QBLOCKS, N_WIDE * CAP)], axis=1)
    all_live = jnp.concatenate([own_live, remote_live.reshape(QBLOCKS, N_WIDE * CAP)], axis=1)
    length_all = 3 + N_WIDE * CAP
    order_keys = jnp.where(all_live, 0, 1) * length_all + jnp.arange(length_all, dtype=jnp.int32)[None, :]
    order = jnp.argsort(order_keys, axis=1, stable=True)[:, :KMAX]
    sorted_ids = jnp.take_along_axis(all_ids, order, axis=1)
    sorted_live = jnp.take_along_axis(all_live, order, axis=1)
    listed = jnp.where(sorted_live, sorted_ids, row_ids[:, None]).astype(jnp.int32)
    counts = jnp.sum(all_live.astype(jnp.int32), axis=1).astype(jnp.int32)
    return (listed, counts)


def draw_key_lists(key, part):
    listed, counts = block_lists(key)
    return listed


def draw_key_counts(key, part):
    listed, counts = block_lists(key)
    return counts


def block_scale(own_key, dims, cuts, smallest, largest):
    def one(position, blocks):
        heights = jax.random.uniform(jax.random.fold_in(jax.random.fold_in(own_key, 6), position), (blocks,), jnp.float32, smallest / len(cuts), largest / len(cuts))
        return jnp.repeat(jnp.exp(heights), dims[position] // blocks).reshape((-1,) + (1,) * (len(dims) - position - 1))

    gain = one(*cuts[0])
    for cut in cuts[1:]:
        gain = gain * one(*cut)
    return gain


def bell_draw(rng, shape, spread, most, shards=(), held_as=jnp.bfloat16):
    values = jax.random.normal(rng, shape, jnp.float32) * spread
    if len(shards) > 0:
        values = block_scale(rng, shape, shards, -0.22, 0.18) * values
    return jnp.clip(values, min=-most, max=most).astype(held_as)


def setup_inputs(seed: int = 0) -> dict:
    key_of = jax.random.split(jax.random.key(seed), 7)
    query_proj = draw_query_proj(jax.random.fold_in(key_of[6], 71), 0)
    key_proj = draw_key_proj(jax.random.fold_in(key_of[6], 71), 0)
    value_proj = bell_draw(key_of[2], (TOKENS, HEADS * HD), 1.0, 6.0, ((0, 128),))
    positions = draw_positions(jax.random.fold_in(key_of[6], 71), 0)
    key_lists = draw_key_lists(jax.random.fold_in(key_of[6], 71), 0)
    key_counts = draw_key_counts(jax.random.fold_in(key_of[6], 71), 0)
    return dict(query_proj=query_proj, key_proj=key_proj, value_proj=value_proj, positions=positions, key_lists=key_lists, key_counts=key_counts)


def rotate(values, positions):
    head_dim = values.shape[-1]
    first_size = head_dim // 4
    second_size = 3 * head_dim // 8
    bounds = (0, first_size, first_size + second_size, head_dim)
    pieces = []
    for axis_row in range(3):
        begin_at = bounds[axis_row]
        end_at = bounds[axis_row + 1]
        section = end_at - begin_at
        half_size = section // 2
        inverse_freq = 10000.0 ** (-2.0 * jnp.arange(half_size, dtype=jnp.float32) / section)
        angles = positions[axis_row].astype(jnp.float32)[:, None] * inverse_freq[None, :]
        cosine = jnp.cos(angles)[:, None, :]
        sines = jnp.sin(angles)[:, None, :]
        lower_half = values[..., begin_at:begin_at + half_size]
        upper_half = values[..., begin_at + half_size:end_at]
        pieces.append(lower_half * cosine - upper_half * sines)
        pieces.append(upper_half * cosine + lower_half * sines)
    return jnp.concatenate(pieces, axis=-1)


def reference(query_proj, key_proj, value_proj, positions, key_lists, key_counts):
    scale = HD ** -0.5
    q_rot = rotate(query_proj.astype(jnp.float32).reshape(TOKENS, HEADS, HD), positions).astype(jnp.bfloat16)
    k_rot = rotate(key_proj.astype(jnp.float32).reshape(TOKENS, HEADS, HD), positions).astype(jnp.bfloat16)
    query_blocks = q_rot.reshape(QBLOCKS, BLOCK, HEADS, HD)
    key_blocks = k_rot.reshape(QBLOCKS, BLOCK, HEADS, HD)
    value_blocks = value_proj.reshape(QBLOCKS, BLOCK, HEADS, HD)

    def attend(row_block):
        listed = key_lists[row_block].astype(jnp.int32)
        live = jnp.arange(KMAX, dtype=jnp.int32) < key_counts[row_block]
        key_rows = key_blocks[listed].astype(jnp.float32).reshape(KMAX * BLOCK, HEADS, HD)
        value_rows = value_blocks[listed].astype(jnp.float32).reshape(KMAX * BLOCK, HEADS, HD)
        scores = jnp.einsum("qhd,khd->hqk", query_blocks[row_block].astype(jnp.float32), key_rows) * scale
        live_keys = jnp.repeat(live, BLOCK)
        scores = jnp.where(live_keys[None, None, :], scores, -jnp.inf)
        row_max = jnp.max(scores, axis=-1, keepdims=True)
        weights = jnp.exp(scores - row_max)
        row_total = jnp.sum(weights, axis=-1)
        weights_low = lax.optimization_barrier(weights.astype(jnp.bfloat16)).astype(jnp.float32)
        mixed = jnp.einsum("hqk,khd->qhd", weights_low, value_rows)
        mixed = mixed / jnp.transpose(row_total)[:, :, None]
        return mixed.astype(jnp.bfloat16)

    attended = lax.map(attend, jnp.arange(QBLOCKS, dtype=jnp.int32))
    return attended.reshape(TOKENS, HEADS * HD)
```

```python
import functools
import math

import jax
import jax.numpy as jnp
import numpy as np
from jax import lax
from jax.experimental import pallas as pl
from jax.experimental.pallas import tpu as pltpu
from jax.sharding import PartitionSpec as P

HEADS = 16
HD = 128
BLOCK = 128
KMAX = 24
MIN_LISTED = 6
F32 = jnp.float32
BF16 = jnp.bfloat16
TO_EXP2 = HD**-0.5 * math.log2(math.e)
SECTIONS = ((0, 32), (32, 80), (80, 128))
ROWS_BY_COLS = (((1,), (0,)), ((), ()))
ROWS_BY_ROWS = (((1,), (1,)), ((), ()))


def pair_matrix():
    pairs = np.zeros((HD, HD), np.float32)
    for begin, end in SECTIONS:
        half = (end - begin) // 2
        for j in range(half):
            pairs[begin + half + j, begin + j] = -1.0
            pairs[begin + j, begin + half + j] = 1.0
    return pairs


def lane_frequencies():
    pieces = []
    for begin, end in SECTIONS:
        section = end - begin
        half = section // 2
        inverse = 10000.0 ** (-2.0 * jnp.arange(half, dtype=F32) / section)
        pieces += [inverse, inverse]
    return jnp.concatenate(pieces)


def rope_kernel(pos_ref, freq_ref, pairs_ref, x_ref, out_ref):
    angles = lax.dot_general(
        pos_ref[...].astype(F32),
        freq_ref[...],
        (((0,), (0,)), ((), ())),
        precision=lax.Precision.HIGHEST,
        preferred_element_type=F32,
    )
    cosine = jnp.cos(angles)
    sine = jnp.sin(angles)
    for head in range(HEADS):
        x = x_ref[:, head * HD : (head + 1) * HD]
        partner = lax.dot_general(x, pairs_ref[...], ROWS_BY_COLS, preferred_element_type=F32)
        out_ref[head] = (x.astype(F32) * cosine + partner * sine).astype(BF16)


def rope(x, positions, freqs, pairs):
    rows = x.shape[0]
    return pl.pallas_call(
        rope_kernel,
        out_shape=jax.ShapeDtypeStruct((HEADS, rows, HD), BF16),
        compiler_params=pltpu.CompilerParams(vmem_limit_bytes=24 * 2**20),
        name="rope",
    )(positions, freqs, pairs, x)


def attend_kernel(
    lists_ref, counts_ref, q_ref, k_hbm, v_hbm, out_ref, k_ref, v_ref, s_ref, m_ref, sems
):
    blocks = q_ref.shape[0]
    pair_count = KMAX // 2
    k_copy = pltpu.make_async_copy(k_hbm, k_ref, sems.at[0])
    v_copy = pltpu.make_async_copy(v_hbm, v_ref, sems.at[1])
    k_copy.start()
    v_copy.start()
    k_copy.wait()
    v_copy.wait()

    def pair_of(ref, row, pair):
        at = row * KMAX + 2 * pair
        return jnp.concatenate([ref[lists_ref[at]], ref[lists_ref[at + 1]]], axis=0)

    def step(row, carry):
        query = q_ref[row]
        largest = None
        for pair in range(pair_count):
            scores = lax.dot_general(
                query, pair_of(k_ref, row, pair), ROWS_BY_ROWS, preferred_element_type=F32
            )
            s_ref[pair] = scores
            for half in range(2):
                part = scores[:, half * BLOCK : (half + 1) * BLOCK]
                largest = part if largest is None else jnp.maximum(largest, part)
        shift = jnp.broadcast_to(
            jnp.max(largest, axis=1, keepdims=True) * TO_EXP2, (BLOCK, BLOCK)
        )
        count = counts_ref[row]
        total = None
        mixed = None
        for pair in range(pair_count):
            weights = []
            for half in range(2):
                entry = 2 * pair + half
                shift_here = shift
                if entry >= MIN_LISTED:
                    shift_here = shift + jnp.where(entry < count, 0.0, 1e30)
                part = jnp.exp2(
                    s_ref[pair, :, half * BLOCK : (half + 1) * BLOCK] * TO_EXP2 - shift_here
                )
                total = part if total is None else total + part
                weights.append(part.astype(BF16))
            product = lax.dot_general(
                jnp.concatenate(weights, axis=1),
                pair_of(v_ref, row, pair),
                ROWS_BY_COLS,
                preferred_element_type=F32,
            )
            mixed = product if mixed is None else mixed + product
        out_ref[row] = (mixed / jnp.sum(total, axis=1, keepdims=True)).astype(BF16)
        return carry

    lax.fori_loop(0, blocks, step, 0)


def attend(lists, counts, q, k, v):
    blocks = q.shape[0]
    all_blocks = k.shape[0]
    whole = pl.BlockSpec((blocks, BLOCK, HD), lambda g, *_: (0, 0, 0))
    anywhere = pl.BlockSpec(memory_space=pl.ANY)
    return pl.pallas_call(
        attend_kernel,
        grid_spec=pltpu.PrefetchScalarGridSpec(
            num_scalar_prefetch=2,
            grid=(1,),
            in_specs=[whole, anywhere, anywhere],
            out_specs=whole,
            scratch_shapes=[
                pltpu.VMEM((all_blocks, BLOCK, HD), BF16),
                pltpu.VMEM((all_blocks, BLOCK, HD), BF16),
                pltpu.VMEM((KMAX // 2, BLOCK, 2 * BLOCK), F32),
                pltpu.VMEM((8, BLOCK), F32),
                pltpu.SemaphoreType.DMA((2,)),
            ],
        ),
        out_shape=jax.ShapeDtypeStruct((blocks, BLOCK, HD), BF16),
        compiler_params=pltpu.CompilerParams(vmem_limit_bytes=48 * 2**20),
        name="attend",
    )(lists, counts, q, k, v)


def shards(query_proj, key_proj, value_proj, positions, key_lists, key_counts):
    frames = lax.axis_size("wide")
    parts = lax.axis_size("narrow")
    part = lax.axis_index("narrow")
    rows = query_proj.shape[0]
    halves = rows // BLOCK
    frame_blocks = parts * halves

    lane = np.arange(HD)
    axis_of = np.searchsorted([32, 80], lane, side="right")
    freqs = jnp.where(
        jnp.asarray(axis_of[None, :] == np.arange(3)[:, None]), lane_frequencies()[None, :], 0.0
    )
    pairs = jnp.asarray(pair_matrix(), BF16)

    def heads_out(x):
        return lax.all_to_all(x, "wide", split_axis=0, concat_axis=0, tiled=True)

    def all_parts(x):
        return lax.all_gather(x, "narrow", axis=0).reshape(
            parts * frames * halves, BLOCK, HD
        )

    k_all = all_parts(heads_out(rope(key_proj, positions, freqs, pairs)))
    v_heads = value_proj.reshape(rows, HEADS, HD).transpose(1, 0, 2)
    v_all = all_parts(heads_out(v_heads))
    q = heads_out(rope(query_proj, positions, freqs, pairs)).reshape(frames * halves, BLOCK, HD)

    frame = key_lists // frame_blocks
    inner = key_lists % frame_blocks
    places = (inner // halves) * (frames * halves) + frame * halves + inner % halves
    mine = lax.dynamic_index_in_dim(
        places.reshape(frames, parts, halves * KMAX), part, 1, keepdims=False
    ).reshape(-1)
    counts = lax.dynamic_index_in_dim(
        key_counts.reshape(frames, parts, halves), part, 1, keepdims=False
    ).reshape(-1)

    mixed = attend(mine, counts, q, k_all, v_all).reshape(frames, rows, HD)
    back = heads_out(mixed)
    return back.transpose(1, 0, 2).reshape(rows, HEADS * HD)


def solution(mesh):
    return jax.shard_map(
        shards,
        mesh=mesh,
        in_specs=(
            P(("wide", "narrow"), None),
            P(("wide", "narrow"), None),
            P(("wide", "narrow"), None),
            P(None, ("wide", "narrow")),
            P(),
            P(),
        ),
        out_specs=P(("wide", "narrow"), None),
        check_vma=False,
    )
```

```python
import functools
import math

import jax
import jax.numpy as jnp
import numpy as np
from jax import lax
from jax.experimental import pallas as pl
from jax.experimental.pallas import tpu as pltpu
from jax.sharding import PartitionSpec as P

HEADS = 16
HD = 128
BLOCK = 128
KMAX = 24
MIN_LISTED = 6
F32 = jnp.float32
BF16 = jnp.bfloat16
TO_EXP2 = HD**-0.5 * math.log2(math.e)
SECTIONS = ((0, 32), (32, 80), (80, 128))
ROWS_BY_COLS = (((1,), (0,)), ((), ()))
ROWS_BY_ROWS = (((1,), (1,)), ((), ()))


def pair_matrix():
    pairs = np.zeros((HD, HD), np.float32)
    for begin, end in SECTIONS:
        half = (end - begin) // 2
        for j in range(half):
            pairs[begin + half + j, begin + j] = -1.0
            pairs[begin + j, begin + half + j] = 1.0
    return pairs


def lane_frequencies():
    pieces = []
    for begin, end in SECTIONS:
        section = end - begin
        half = section // 2
        inverse = 10000.0 ** (-2.0 * jnp.arange(half, dtype=F32) / section)
        pieces += [inverse, inverse]
    return jnp.concatenate(pieces)


def rope_kernel(pos_ref, freq_ref, pairs_ref, x_ref, out_ref):
    angles = lax.dot_general(
        pos_ref[...].astype(F32),
        freq_ref[...],
        (((0,), (0,)), ((), ())),
        precision=lax.Precision.HIGHEST,
        preferred_element_type=F32,
    )
    cosine = jnp.cos(angles)
    sine = jnp.sin(angles)
    for head in range(HEADS):
        x = x_ref[:, head * HD : (head + 1) * HD]
        partner = lax.dot_general(x, pairs_ref[...], ROWS_BY_COLS, preferred_element_type=F32)
        out_ref[head] = (x.astype(F32) * cosine + partner * sine).astype(BF16)


def rope(x, positions, freqs, pairs):
    rows = x.shape[0]
    return pl.pallas_call(
        rope_kernel,
        out_shape=jax.ShapeDtypeStruct((HEADS, rows, HD), BF16),
        compiler_params=pltpu.CompilerParams(vmem_limit_bytes=24 * 2**20),
        name="rope",
    )(positions, freqs, pairs, x)


def load_blocks(sources, target, sems):
    copies = []
    at = 0
    for n, source in enumerate(sources):
        blocks = source.shape[0]
        copies.append(pltpu.make_async_copy(source, target.at[pl.ds(at, blocks)], sems.at[n]))
        at += blocks
    for copy in copies:
        copy.start()
    for copy in copies:
        copy.wait()


def listed_pair(ref, lists_ref, row, pair):
    at = row * KMAX + 2 * pair
    return jnp.concatenate([ref[lists_ref[at]], ref[lists_ref[at + 1]]], axis=0)


def weights_kernel(sources, unroll, lists_ref, counts_ref, q_ref, *refs):
    k_parts = refs[:sources]
    weights_ref, inverse_ref, k_ref, s_ref, sems = refs[sources:]
    load_blocks(k_parts, k_ref, sems)

    def row_weights(row, turn):
        query = q_ref[row]
        largest = None
        for pair in range(KMAX // 2):
            scores = lax.dot_general(
                query,
                listed_pair(k_ref, lists_ref, row, pair),
                ROWS_BY_ROWS,
                preferred_element_type=F32,
            )
            s_ref[turn, pair] = scores
            for half in range(2):
                part = scores[:, half * BLOCK : (half + 1) * BLOCK]
                largest = part if largest is None else jnp.maximum(largest, part)
        shift = jnp.broadcast_to(
            jnp.max(largest, axis=1, keepdims=True) * TO_EXP2, (BLOCK, BLOCK)
        )
        count = counts_ref[row]
        total = None
        for entry in range(KMAX):
            pair, half = divmod(entry, 2)
            shift_here = shift
            if entry >= MIN_LISTED:
                shift_here = shift + jnp.where(entry < count, 0.0, 1e30)
            lanes = slice(half * BLOCK, (half + 1) * BLOCK)
            part = jnp.exp2(s_ref[turn, pair, :, lanes] * TO_EXP2 - shift_here)
            total = part if total is None else total + part
            weights_ref[row, pair, :, lanes] = part.astype(BF16)
        inverse_ref[row] = jnp.broadcast_to(
            1.0 / jnp.sum(total, axis=1, keepdims=True), (BLOCK, BLOCK)
        )

    def step(turn, carry):
        for n in range(unroll):
            row_weights(turn * unroll + n, n)
        return carry

    lax.fori_loop(0, q_ref.shape[0] // unroll, step, 0)


SMEM_SPEC = pl.BlockSpec(memory_space=pltpu.SMEM)
VMEM_SPEC = pl.BlockSpec(memory_space=pltpu.VMEM)
ANY_SPEC = pl.BlockSpec(memory_space=pl.ANY)


def weights_of(lists, counts, q, k_parts, unroll=4):
    rows = q.shape[0]
    blocks = sum(part.shape[0] for part in k_parts)
    return pl.pallas_call(
        functools.partial(weights_kernel, len(k_parts), unroll),
        in_specs=[SMEM_SPEC, SMEM_SPEC, VMEM_SPEC] + [ANY_SPEC] * len(k_parts),
        out_specs=[VMEM_SPEC, VMEM_SPEC],
        scratch_shapes=[
            pltpu.VMEM((blocks, BLOCK, HD), BF16),
            pltpu.VMEM((unroll, KMAX // 2, BLOCK, 2 * BLOCK), F32),
            pltpu.SemaphoreType.DMA((len(k_parts),)),
        ],
        out_shape=[
            pltpu.VMEM((rows, KMAX // 2, BLOCK, 2 * BLOCK), BF16),
            pltpu.VMEM((rows, BLOCK, BLOCK), F32),
        ],
        compiler_params=pltpu.CompilerParams(vmem_limit_bytes=20 * 2**20),
        name="weights",
    )(lists, counts, q, *k_parts)


def mix_of(lists, halves, v_parts, unroll=8):
    rows = sum(weights.shape[0] for weights, _ in halves)
    blocks = sum(part.shape[0] for part in v_parts)

    def kernel(lists_ref, *refs):
        groups = [refs[2 * n : 2 * n + 2] for n in range(len(halves))]
        v_refs = refs[2 * len(halves) : 2 * len(halves) + len(v_parts)]
        out_ref, v_ref, sems = refs[2 * len(halves) + len(v_parts) :]
        load_blocks(v_refs, v_ref, sems)
        first = 0
        for weights_ref, inverse_ref in groups:

            def step(turn, carry, weights_ref=weights_ref, inverse_ref=inverse_ref, first=first):
                for n in range(unroll):
                    row = turn * unroll + n
                    mixed = None
                    for pair in range(KMAX // 2):
                        product = lax.dot_general(
                            weights_ref[row, pair],
                            listed_pair(v_ref, lists_ref, first + row, pair),
                            ROWS_BY_COLS,
                            preferred_element_type=F32,
                        )
                        mixed = product if mixed is None else mixed + product
                    out_ref[first + row] = (mixed * inverse_ref[row]).astype(BF16)
                return carry

            lax.fori_loop(0, weights_ref.shape[0] // unroll, step, 0)
            first += weights_ref.shape[0]

    return pl.pallas_call(
        kernel,
        in_specs=[SMEM_SPEC] + [VMEM_SPEC] * (2 * len(halves)) + [ANY_SPEC] * len(v_parts),
        out_specs=VMEM_SPEC,
        scratch_shapes=[
            pltpu.VMEM((blocks, BLOCK, HD), BF16),
            pltpu.SemaphoreType.DMA((len(v_parts),)),
        ],
        out_shape=jax.ShapeDtypeStruct((rows, BLOCK, HD), BF16),
        compiler_params=pltpu.CompilerParams(vmem_limit_bytes=14 * 2**20),
        name="mix",
    )(lists, *[ref for pair in halves for ref in pair], *v_parts)


def around(own):
    chips = lax.axis_size("narrow") // 2

    def along(x):
        steps = [(2 * z, 2 * ((z + 1) % chips)) for z in range(chips)]
        steps += [(2 * z + 1, 2 * ((z - 1) % chips) + 1) for z in range(chips)]
        return lax.ppermute(x, "narrow", steps)

    def across(x):
        return lax.ppermute(x, "narrow", [(n, n ^ 1) for n in range(2 * chips)])

    near_same = along(own)
    other = across(own)
    near_other = along(other)
    far_same = along(near_same)
    side_other = across(near_same)
    side_same = across(near_other)
    far_other = across(far_same)
    return [own, other, near_same, near_other, far_same, far_other, side_other, side_same]


def slots_of(source, part, chips):
    chip, core = part // 2, part % 2
    apart = (source // 2 - chip) % chips
    same = (source % 2) == core
    near = jnp.where(core == 0, chips - 1, 1)
    slot = jnp.where(same, 7, 6)
    slot = jnp.where(apart == near, jnp.where(same, 2, 3), slot)
    slot = jnp.where(apart == 2, jnp.where(same, 4, 5), slot)
    return jnp.where(apart == 0, jnp.where(same, 0, 1), slot)


def shards(query_proj, key_proj, value_proj, positions, key_lists, key_counts):
    frames = lax.axis_size("wide")
    parts = lax.axis_size("narrow")
    part = lax.axis_index("narrow")
    rows = query_proj.shape[0]
    halves = rows // BLOCK
    frame_blocks = parts * halves

    lane = np.arange(HD)
    axis_of = np.searchsorted([32, 80], lane, side="right")
    freqs = jnp.where(
        jnp.asarray(axis_of[None, :] == np.arange(3)[:, None]), lane_frequencies()[None, :], 0.0
    )
    pairs = jnp.asarray(pair_matrix(), BF16)

    def heads_out(x):
        return lax.all_to_all(x, "wide", split_axis=0, concat_axis=0, tiled=True)

    def blocks_of(x):
        return x.reshape(frames * halves, BLOCK, HD)

    k_heads = heads_out(rope(key_proj, positions, freqs, pairs))
    v_heads = heads_out(value_proj.reshape(rows, HEADS, HD).transpose(1, 0, 2))
    q_heads = heads_out(rope(query_proj, positions, freqs, pairs))
    k_parts = [blocks_of(x) for x in around(k_heads)]
    v_parts = [blocks_of(x) for x in around(v_heads)]
    q = blocks_of(q_heads)

    frame = key_lists // frame_blocks
    inner = key_lists % frame_blocks
    slot = slots_of(inner // halves, part, parts // 2)
    places = slot * (frames * halves) + frame * halves + inner % halves
    mine = lax.dynamic_index_in_dim(
        places.reshape(frames, parts, halves * KMAX), part, 1, keepdims=False
    ).reshape(-1)
    counts = lax.dynamic_index_in_dim(
        key_counts.reshape(frames, parts, halves), part, 1, keepdims=False
    ).reshape(-1)

    half = frames * halves // 2
    first = weights_of(mine[: half * KMAX], counts[:half], q[:half], k_parts)
    second = weights_of(mine[half * KMAX :], counts[half:], q[half:], k_parts)
    mixed = mix_of(mine, [first, second], v_parts).reshape(frames, rows, HD)
    back = heads_out(mixed)
    return back.transpose(1, 0, 2).reshape(rows, HEADS * HD)


def solution(mesh):
    return jax.shard_map(
        shards,
        mesh=mesh,
        in_specs=(
            P(("wide", "narrow"), None),
            P(("wide", "narrow"), None),
            P(("wide", "narrow"), None),
            P(None, ("wide", "narrow")),
            P(),
            P(),
        ),
        out_specs=P(("wide", "narrow"), None),
        check_vma=False,
    )
```

```python
import functools
import math

import jax
import jax.numpy as jnp
from jax import lax
from jax.experimental import pallas as pl
from jax.experimental.pallas import tpu as pltpu
from jax.sharding import PartitionSpec as P

HEADS = 16
HD = 128
BLOCK = 128
KMAX = 24
MIN_LISTED = 6
F32 = jnp.float32
BF16 = jnp.bfloat16
TO_EXP2 = HD**-0.5 * math.log2(math.e)
SECTIONS = ((0, 32), (32, 80), (80, 128))
ROWS_BY_COLS = (((1,), (0,)), ((), ()))
ROWS_BY_ROWS = (((1,), (1,)), ((), ()))


def section_of(lane):
    second = lane >= SECTIONS[1][0]
    third = lane >= SECTIONS[2][0]
    begin = jnp.where(third, SECTIONS[2][0], jnp.where(second, SECTIONS[1][0], 0))
    length = jnp.where(second, SECTIONS[1][1] - SECTIONS[1][0], SECTIONS[0][1])
    number = jnp.where(third, 2, jnp.where(second, 1, 0))
    return begin, length, number


def rotation_of(pos_ref):
    lane = lax.broadcasted_iota(jnp.int32, (3, HD), 1)
    begin, length, number = section_of(lane)
    half = lax.shift_right_logical(length, 1)
    at = lane - begin
    at = jnp.where(at >= half, at - half, at)
    exponent = at.astype(F32) * (-2.0 * math.log(10000.0)) / length.astype(F32)
    mine = number == lax.broadcasted_iota(jnp.int32, (3, HD), 0)
    freqs = jnp.where(mine, jnp.exp(exponent), 0.0)
    angles = lax.dot_general(
        pos_ref[...].astype(F32),
        freqs,
        (((0,), (0,)), ((), ())),
        precision=lax.Precision.HIGHEST,
        preferred_element_type=F32,
    )
    source = lax.broadcasted_iota(jnp.int32, (HD, HD), 0)
    target = lax.broadcasted_iota(jnp.int32, (HD, HD), 1)
    begin, length, number = section_of(target)
    half = lax.shift_right_logical(length, 1)
    lower = target - begin < half
    partner = jnp.where(lower, target + half, target - half)
    sign = jnp.where(lower, -1.0, 1.0)
    pairs = jnp.where(source == partner, sign, 0.0).astype(BF16)
    return jnp.cos(angles), jnp.sin(angles), pairs


def rotate_heads(x_ref, out_ref, cosine, sine, pairs):
    for head in range(HEADS):
        x = x_ref[:, head * HD : (head + 1) * HD]
        partner = lax.dot_general(x, pairs, ROWS_BY_COLS, preferred_element_type=F32)
        out_ref[head] = (x.astype(F32) * cosine + partner * sine).astype(BF16)


def keys_kernel(pos_ref, k_ref, out_ref):
    rotate_heads(k_ref, out_ref, *rotation_of(pos_ref))


def others_kernel(pos_ref, q_ref, v_ref, q_out, v_out):
    for head in range(HEADS):
        v_out[head] = v_ref[:, head * HD : (head + 1) * HD]
    rotate_heads(q_ref, q_out, *rotation_of(pos_ref))


def by_heads(kernel, name, positions, *xs):
    heads = jax.ShapeDtypeStruct((HEADS, xs[0].shape[0], HD), BF16)
    return pl.pallas_call(
        kernel,
        out_shape=[heads] * len(xs),
        compiler_params=pltpu.CompilerParams(vmem_limit_bytes=50 * 2**20),
        name=name,
    )(positions, *xs)


def load_blocks(sources, target, sems, then=()):
    copies = []
    at = 0
    for n, source in enumerate(sources):
        blocks = source.shape[0]
        copies.append(pltpu.make_async_copy(source, target.at[pl.ds(at, blocks)], sems.at[n]))
        at += blocks
    for copy in copies:
        copy.start()
    for copy in then:
        copy.start()
    for copy in copies:
        copy.wait()


def listed_pair(ref, lists_ref, row, pair):
    at = row * KMAX + 2 * pair
    return jnp.concatenate([ref[lists_ref[at]], ref[lists_ref[at + 1]]], axis=0)


def weights_kernel(sources, unroll, first, rows, lists_ref, counts_ref, q_ref, *refs):
    k_parts = refs[:sources]
    weights_out, inverse_ref, k_ref, s_ref, w_ref, sems, out_sems = refs[sources:]
    load_blocks(k_parts, k_ref, sems)
    turns = rows // unroll

    def leave(turn, slot):
        return pltpu.make_async_copy(
            w_ref.at[slot], weights_out.at[pl.ds(turn * unroll, unroll)], out_sems.at[slot]
        )

    def row_weights(row, slot, n):
        query = q_ref[first + row]
        largest = None
        for pair in range(KMAX // 2):
            scores = lax.dot_general(
                query,
                listed_pair(k_ref, lists_ref, first + row, pair),
                ROWS_BY_ROWS,
                preferred_element_type=F32,
            )
            s_ref[n, pair] = scores
            for half in range(2):
                part = scores[:, half * BLOCK : (half + 1) * BLOCK]
                largest = part if largest is None else jnp.maximum(largest, part)
        shift = jnp.broadcast_to(
            jnp.max(largest, axis=1, keepdims=True) * TO_EXP2, (BLOCK, BLOCK)
        )
        count = counts_ref[first + row]
        total = None
        for entry in range(KMAX):
            pair, half = divmod(entry, 2)
            shift_here = shift
            if entry >= MIN_LISTED:
                shift_here = shift + jnp.where(entry < count, 0.0, 1e30)
            lanes = slice(half * BLOCK, (half + 1) * BLOCK)
            part = jnp.exp2(s_ref[n, pair, :, lanes] * TO_EXP2 - shift_here)
            total = part if total is None else total + part
            w_ref[slot, n, pair, :, lanes] = part.astype(BF16)
        inverse_ref[row] = jnp.broadcast_to(
            1.0 / jnp.sum(total, axis=1, keepdims=True), (BLOCK, BLOCK)
        )

    def step(turn, carry):
        slot = turn & 1

        @pl.when(turn >= 2)
        def _():
            leave(turn - 2, slot).wait()

        for n in range(unroll):
            row_weights(turn * unroll + n, slot, n)
        leave(turn, slot).start()
        return carry

    lax.fori_loop(0, turns, step, 0)
    for turn in range(max(turns - 2, 0), turns):
        leave(turn, turn & 1).wait()


SMEM_SPEC = pl.BlockSpec(memory_space=pltpu.SMEM)
VMEM_SPEC = pl.BlockSpec(memory_space=pltpu.VMEM)
ANY_SPEC = pl.BlockSpec(memory_space=pl.ANY)


def weights_of(lists, counts, q, k_parts, first, rows, unroll=4):
    blocks = sum(part.shape[0] for part in k_parts)
    group = (unroll, KMAX // 2, BLOCK, 2 * BLOCK)
    return pl.pallas_call(
        functools.partial(weights_kernel, len(k_parts), unroll, first, rows),
        in_specs=[SMEM_SPEC, SMEM_SPEC, VMEM_SPEC] + [ANY_SPEC] * len(k_parts),
        out_specs=[ANY_SPEC, VMEM_SPEC],
        scratch_shapes=[
            pltpu.VMEM((blocks, BLOCK, HD), BF16),
            pltpu.VMEM(group, F32),
            pltpu.VMEM((2,) + group, BF16),
            pltpu.SemaphoreType.DMA((len(k_parts),)),
            pltpu.SemaphoreType.DMA((2,)),
        ],
        out_shape=[
            jax.ShapeDtypeStruct((rows,) + group[1:], BF16),
            jax.ShapeDtypeStruct((rows, BLOCK, BLOCK), F32),
        ],
        compiler_params=pltpu.CompilerParams(vmem_limit_bytes=48 * 2**20),
        cost_estimate=pl.CostEstimate(
            flops=2 * rows * KMAX * BLOCK * BLOCK * HD,
            bytes_accessed=rows * 3 * 2**20,
            transcendentals=rows * KMAX * BLOCK * BLOCK,
        ),
        name="weights",
    )(lists, counts, q, *k_parts)


def mix_of(lists, halves, v_parts, unroll=4, slots=4):
    groups = len(halves)
    group_rows = halves[0][0].shape[0]
    rows = groups * group_rows
    turns = rows // unroll
    blocks = sum(part.shape[0] for part in v_parts)

    def kernel(lists_ref, *refs):
        weights_refs = refs[:groups]
        inverse_refs = refs[groups : 2 * groups]
        v_refs = refs[2 * groups : 2 * groups + len(v_parts)]
        out_ref, v_ref, w_ref, sems, w_sems = refs[2 * groups + len(v_parts) :]

        def fetch(turn):
            group, at = divmod(turn * unroll, group_rows)
            slot = turn % slots
            return pltpu.make_async_copy(
                weights_refs[group].at[pl.ds(at, unroll)], w_ref.at[slot], w_sems.at[slot]
            )

        fetch(0).start()
        load_blocks(v_refs, v_ref, sems, [fetch(n) for n in range(1, slots - 1)])
        for turn in range(turns):
            fetch(turn).wait()
            if turn + slots - 1 < turns:
                fetch(turn + slots - 1).start()
            for n in range(unroll):
                row = turn * unroll + n
                group, at = divmod(row, group_rows)
                mixed = None
                for pair in range(KMAX // 2):
                    product = lax.dot_general(
                        w_ref[turn % slots, n, pair],
                        listed_pair(v_ref, lists_ref, row, pair),
                        ROWS_BY_COLS,
                        preferred_element_type=F32,
                    )
                    mixed = product if mixed is None else mixed + product
                out_ref[row] = (mixed * inverse_refs[group][at]).astype(BF16)

    return pl.pallas_call(
        kernel,
        in_specs=[SMEM_SPEC]
        + [ANY_SPEC] * groups
        + [VMEM_SPEC] * groups
        + [ANY_SPEC] * len(v_parts),
        out_specs=VMEM_SPEC,
        scratch_shapes=[
            pltpu.VMEM((blocks, BLOCK, HD), BF16),
            pltpu.VMEM((slots, unroll, KMAX // 2, BLOCK, 2 * BLOCK), BF16),
            pltpu.SemaphoreType.DMA((len(v_parts),)),
            pltpu.SemaphoreType.DMA((slots,)),
        ],
        out_shape=jax.ShapeDtypeStruct((rows, BLOCK, HD), BF16),
        compiler_params=pltpu.CompilerParams(vmem_limit_bytes=48 * 2**20),
        cost_estimate=pl.CostEstimate(
            flops=2 * rows * KMAX * BLOCK * BLOCK * HD,
            bytes_accessed=rows * 3 * 2**19,
            transcendentals=0,
        ),
        name="mix",
    )(lists, *[w for w, _ in halves], *[i for _, i in halves], *v_parts)


def after(x, *others):
    return lax.optimization_barrier((x,) + others)[0]


class Ring:
    def __init__(self):
        self.chips = lax.axis_size("narrow") // 2

    def along(self, x, turn):
        steps = [
            (2 * z + core, 2 * ((z + (turn if core == 0 else -turn)) % self.chips) + core)
            for z in range(self.chips)
            for core in range(2)
        ]
        return lax.ppermute(x, "narrow", steps)

    def across(self, x):
        return lax.ppermute(x, "narrow", [(n, n ^ 1) for n in range(2 * self.chips)])


def slots_of(source, part):
    core = part & 1
    apart = (lax.shift_right_logical(source, 1) - lax.shift_right_logical(part, 1)) & 3
    same = (source & 1) == core
    main = jnp.where(core == 0, 3, 1)
    slot_same = jnp.where(apart == 0, 0, jnp.where(apart == 2, 3, jnp.where(apart == main, 1, 2)))
    slot_other = jnp.where(apart == 0, 4, jnp.where(apart == 2, 7, jnp.where(apart == main, 6, 5)))
    return jnp.where(same, slot_same, slot_other)


def shards(query_proj, key_proj, value_proj, positions, key_lists, key_counts):
    frames = lax.axis_size("wide")
    parts = lax.axis_size("narrow")
    part = lax.axis_index("narrow")
    rows = query_proj.shape[0]
    halves = rows // BLOCK
    frame_blocks = parts * halves
    ring = Ring()

    def heads_out(x):
        return lax.all_to_all(x, "wide", split_axis=0, concat_axis=0, tiled=True)

    def blocks_of(x):
        return x.reshape(frames * halves, BLOCK, HD)

    shift = frame_blocks.bit_length() - 1
    frame = lax.shift_right_logical(key_lists, shift)
    inner = key_lists & (frame_blocks - 1)
    source = lax.shift_right_logical(inner, halves.bit_length() - 1)
    places = slots_of(source, part) * (frames * halves) + frame * halves + (inner & (halves - 1))
    mine = lax.dynamic_index_in_dim(
        places.reshape(frames, parts, halves * KMAX), part, 1, keepdims=False
    ).reshape(-1)
    counts = lax.dynamic_index_in_dim(
        key_counts.reshape(frames, parts, halves), part, 1, keepdims=False
    ).reshape(-1)

    (k_rot,) = by_heads(keys_kernel, "rotate_keys", positions, key_proj)
    q_rot, v_heads = by_heads(
        others_kernel, "rotate_queries", after(positions, k_rot), query_proj, value_proj
    )

    k_own = after(heads_out(k_rot), v_heads, mine, counts)
    k_main = ring.along(k_own, 1)
    k_opposite = ring.along(k_own, -1)
    k_other = ring.across(k_own)
    v_own = heads_out(after(v_heads, k_own))
    k_far = ring.along(after(k_main, v_own), 1)
    k_main_other = ring.across(k_main)
    k_opposite_other = ring.across(k_opposite)
    q_heads = heads_out(after(q_rot, v_own, k_main_other))
    q = blocks_of(q_heads)
    k_far_other = ring.across(after(k_far, q_heads))
    k_parts = [k_own, k_main, k_opposite, k_far, k_other, k_main_other, k_opposite_other, k_far_other]
    k_parts = [blocks_of(x) for x in k_parts]


    v_ring = after(v_own, k_main_other)
    v_main = ring.along(v_ring, 1)
    v_opposite = ring.along(v_ring, -1)
    v_other = ring.across(v_ring)

    half = frames * halves // 2
    first = weights_of(mine, counts, q, k_parts, 0, half)
    v_main, v_opposite = lax.optimization_barrier((v_main, v_opposite, first[1]))[:2]
    v_far = ring.along(v_main, 1)
    second = weights_of(after(mine, v_main), counts, q, k_parts, half, half)
    v_parts = [v_own, v_main, v_opposite, v_far, v_other]
    v_parts += [ring.across(x) for x in (v_main, v_opposite, after(v_far, second[1]))]
    v_parts = [blocks_of(x) for x in v_parts]
    mixed = mix_of(mine, [first, second], v_parts).reshape(frames, rows, HD)
    back = heads_out(mixed)
    return back.transpose(1, 0, 2).reshape(rows, HEADS * HD)


def solution(mesh):
    return jax.shard_map(
        shards,
        mesh=mesh,
        in_specs=(
            P(("wide", "narrow"), None),
            P(("wide", "narrow"), None),
            P(("wide", "narrow"), None),
            P(None, ("wide", "narrow")),
            P(),
            P(),
        ),
        out_specs=P(("wide", "narrow"), None),
        check_vma=False,
    )
```

```python
import functools
import math

import jax
import jax.numpy as jnp
from jax import lax
from jax.experimental import pallas as pl
from jax.experimental.pallas import tpu as pltpu
from jax.sharding import PartitionSpec as P

HEADS = 16
HD = 128
BLOCK = 128
KMAX = 24
MIN_LISTED = 6
PIECES = 4
F32 = jnp.float32
BF16 = jnp.bfloat16
TO_EXP2 = HD**-0.5 * math.log2(math.e)
SECTIONS = ((0, 32), (32, 80), (80, 128))
ROWS_BY_COLS = (((1,), (0,)), ((), ()))
ROWS_BY_ROWS = (((1,), (1,)), ((), ()))


def section_of(lane):
    second = lane >= SECTIONS[1][0]
    third = lane >= SECTIONS[2][0]
    begin = jnp.where(third, SECTIONS[2][0], jnp.where(second, SECTIONS[1][0], 0))
    length = jnp.where(second, SECTIONS[1][1] - SECTIONS[1][0], SECTIONS[0][1])
    number = jnp.where(third, 2, jnp.where(second, 1, 0))
    return begin, length, number


def rotation_of(pos_ref):
    lane = lax.broadcasted_iota(jnp.int32, (3, HD), 1)
    begin, length, number = section_of(lane)
    half = lax.shift_right_logical(length, 1)
    at = lane - begin
    at = jnp.where(at >= half, at - half, at)
    exponent = at.astype(F32) * (-2.0 * math.log(10000.0)) / length.astype(F32)
    mine = number == lax.broadcasted_iota(jnp.int32, (3, HD), 0)
    freqs = jnp.where(mine, jnp.exp(exponent), 0.0)
    angles = lax.dot_general(
        pos_ref[...].astype(F32),
        freqs,
        (((0,), (0,)), ((), ())),
        precision=lax.Precision.HIGHEST,
        preferred_element_type=F32,
    )
    source = lax.broadcasted_iota(jnp.int32, (HD, HD), 0)
    target = lax.broadcasted_iota(jnp.int32, (HD, HD), 1)
    begin, length, number = section_of(target)
    half = lax.shift_right_logical(length, 1)
    lower = target - begin < half
    partner = jnp.where(lower, target + half, target - half)
    sign = jnp.where(lower, -1.0, 1.0)
    pairs = jnp.where(source == partner, sign, 0.0).astype(BF16)
    return jnp.cos(angles), jnp.sin(angles), pairs


def rotate_heads(x_ref, out_ref, cosine, sine, pairs, heads):
    for head in heads:
        x = x_ref[:, head * HD : (head + 1) * HD]
        partner = lax.dot_general(x, pairs, ROWS_BY_COLS, preferred_element_type=F32)
        out_ref[head] = (x.astype(F32) * cosine + partner * sine).astype(BF16)


def keys_kernel(pos_hbm, k_hbm, out_ref, pos_ref, k_ref, sems):
    positions = pltpu.make_async_copy(pos_hbm, pos_ref, sems.at[PIECES])
    positions.start()
    width = HEADS // PIECES * HD
    pieces = [
        pltpu.make_async_copy(
            k_hbm.at[:, pl.ds(n * width, width)], k_ref.at[:, pl.ds(n * width, width)], sems.at[n]
        )
        for n in range(PIECES)
    ]
    for piece in pieces:
        piece.start()
    positions.wait()
    rotation = rotation_of(pos_ref)
    for n, piece in enumerate(pieces):
        piece.wait()
        heads = range(n * HEADS // PIECES, (n + 1) * HEADS // PIECES)
        rotate_heads(k_ref, out_ref, *rotation, heads)


def others_kernel(pos_ref, q_ref, v_ref, q_out, v_out):
    for head in range(HEADS):
        v_out[head] = v_ref[:, head * HD : (head + 1) * HD]
    rotate_heads(q_ref, q_out, *rotation_of(pos_ref), range(HEADS))


def keys_by_heads(positions, x):
    rows = x.shape[0]
    hbm = pl.BlockSpec(memory_space=pltpu.HBM)
    return pl.pallas_call(
        keys_kernel,
        in_specs=[hbm, hbm],
        out_shape=jax.ShapeDtypeStruct((HEADS, rows, HD), BF16),
        scratch_shapes=[
            pltpu.VMEM(positions.shape, jnp.int32),
            pltpu.VMEM(x.shape, BF16),
            pltpu.SemaphoreType.DMA((PIECES + 1,)),
        ],
        compiler_params=pltpu.CompilerParams(vmem_limit_bytes=60 * 2**20),
        name="rotate_keys",
    )(positions, x)


def others_by_heads(positions, q, v):
    heads = jax.ShapeDtypeStruct((HEADS, q.shape[0], HD), BF16)
    return pl.pallas_call(
        others_kernel,
        out_shape=[heads, heads],
        compiler_params=pltpu.CompilerParams(vmem_limit_bytes=50 * 2**20),
        name="rotate_queries",
    )(positions, q, v)


def load_blocks(sources, target, sems, then=()):
    copies = []
    at = 0
    for n, source in enumerate(sources):
        blocks = source.shape[0]
        copies.append(pltpu.make_async_copy(source, target.at[pl.ds(at, blocks)], sems.at[n]))
        at += blocks
    for copy in copies:
        copy.start()
    for copy in then:
        copy.start()
    for copy in copies:
        copy.wait()


def listed_pair(ref, lists_ref, row, pair):
    at = row * KMAX + 2 * pair
    return jnp.concatenate([ref[lists_ref[at]], ref[lists_ref[at + 1]]], axis=0)


def weights_kernel(sources, unroll, first, rows, lists_ref, counts_ref, q_ref, *refs):
    if sources:
        k_parts = refs[:sources]
        weights_out, inverse_ref, k_ref, s_ref, w_ref, out_sems, sems = refs[sources:]
        load_blocks(k_parts, k_ref, sems)
    else:
        k_ref, weights_out, inverse_ref, s_ref, w_ref, out_sems = refs
    turns = rows // unroll

    def leave(turn, slot):
        return pltpu.make_async_copy(
            w_ref.at[slot], weights_out.at[pl.ds(turn * unroll, unroll)], out_sems.at[slot]
        )

    def row_weights(row, slot, n):
        query = q_ref[first + row]
        largest = None
        for pair in range(KMAX // 2):
            scores = lax.dot_general(
                query,
                listed_pair(k_ref, lists_ref, first + row, pair),
                ROWS_BY_ROWS,
                preferred_element_type=F32,
            )
            s_ref[n, pair] = scores
            for half in range(2):
                part = scores[:, half * BLOCK : (half + 1) * BLOCK]
                largest = part if largest is None else jnp.maximum(largest, part)
        shift = jnp.broadcast_to(
            jnp.max(largest, axis=1, keepdims=True) * TO_EXP2, (BLOCK, BLOCK)
        )
        count = counts_ref[first + row]
        total = None
        for entry in range(KMAX):
            pair, half = divmod(entry, 2)
            shift_here = shift
            if entry >= MIN_LISTED:
                shift_here = shift + jnp.where(entry < count, 0.0, 1e30)
            lanes = slice(half * BLOCK, (half + 1) * BLOCK)
            part = jnp.exp2(s_ref[n, pair, :, lanes] * TO_EXP2 - shift_here)
            total = part if total is None else total + part
            w_ref[slot, n, pair, :, lanes] = part.astype(BF16)
        inverse_ref[row] = jnp.broadcast_to(
            1.0 / jnp.sum(total, axis=1, keepdims=True), (BLOCK, BLOCK)
        )

    def step(turn, carry):
        slot = turn & 1

        @pl.when(turn >= 2)
        def _():
            leave(turn - 2, slot).wait()

        for n in range(unroll):
            row_weights(turn * unroll + n, slot, n)
        leave(turn, slot).start()
        return carry

    lax.fori_loop(0, turns, step, 0)
    for turn in range(max(turns - 2, 0), turns):
        leave(turn, turn & 1).wait()


SMEM_SPEC = pl.BlockSpec(memory_space=pltpu.SMEM)
VMEM_SPEC = pl.BlockSpec(memory_space=pltpu.VMEM)
ANY_SPEC = pl.BlockSpec(memory_space=pl.ANY)


def part_specs(parts):
    half = len(parts) // 2
    return ([ANY_SPEC] * (half - 1) + [VMEM_SPEC]) * 2


def weights_of(lists, counts, q, k_parts, first, rows, unroll=4):
    whole = not isinstance(k_parts, list)
    parts = [k_parts] if whole else k_parts
    sources = 0 if whole else len(parts)
    blocks = sum(part.shape[0] for part in parts)
    group = (unroll, KMAX // 2, BLOCK, 2 * BLOCK)
    out_shape = [
        pltpu.HBM((rows,) + group[1:], BF16),
        jax.ShapeDtypeStruct((rows, BLOCK, BLOCK), F32),
    ]
    scratch = [
        pltpu.VMEM(group, F32),
        pltpu.VMEM((2,) + group, BF16),
        pltpu.SemaphoreType.DMA((2,)),
    ]
    out_specs = [pl.BlockSpec(memory_space=pltpu.HBM), VMEM_SPEC]
    if not whole:
        out_shape.append(pltpu.VMEM((blocks, BLOCK, HD), BF16))
        out_specs.append(VMEM_SPEC)
        scratch.append(pltpu.SemaphoreType.DMA((sources,)))
    return pl.pallas_call(
        functools.partial(weights_kernel, sources, unroll, first, rows),
        in_specs=[SMEM_SPEC, SMEM_SPEC, VMEM_SPEC] + ([VMEM_SPEC] if whole else part_specs(parts)),
        out_specs=out_specs,
        scratch_shapes=scratch,
        out_shape=out_shape,
        compiler_params=pltpu.CompilerParams(vmem_limit_bytes=20 * 2**20),
        cost_estimate=pl.CostEstimate(
            flops=2 * rows * KMAX * BLOCK * BLOCK * HD,
            bytes_accessed=rows * 3 * 2**20,
            transcendentals=rows * KMAX * BLOCK * BLOCK,
        ),
        name="weights",
    )(lists, counts, q, *parts)


def mix_of(lists, halves, v_parts, unroll=4, slots=4):
    groups = len(halves)
    group_rows = halves[0][0].shape[0]
    rows = groups * group_rows
    turns = rows // unroll
    blocks = sum(part.shape[0] for part in v_parts)

    def kernel(lists_ref, *refs):
        weights_refs = refs[:groups]
        inverse_refs = refs[groups : 2 * groups]
        v_refs = refs[2 * groups : 2 * groups + len(v_parts)]
        out_ref, v_ref, w_ref, sems, w_sems = refs[2 * groups + len(v_parts) :]

        def fetch(turn):
            group, at = divmod(turn * unroll, group_rows)
            slot = turn % slots
            return pltpu.make_async_copy(
                weights_refs[group].at[pl.ds(at, unroll)], w_ref.at[slot], w_sems.at[slot]
            )

        fetch(0).start()
        load_blocks(v_refs, v_ref, sems, [fetch(n) for n in range(1, slots - 1)])
        for turn in range(turns):
            fetch(turn).wait()
            if turn + slots - 1 < turns:
                fetch(turn + slots - 1).start()
            for n in range(unroll):
                row = turn * unroll + n
                group, at = divmod(row, group_rows)
                mixed = None
                for pair in range(KMAX // 2):
                    product = lax.dot_general(
                        w_ref[turn % slots, n, pair],
                        listed_pair(v_ref, lists_ref, row, pair),
                        ROWS_BY_COLS,
                        preferred_element_type=F32,
                    )
                    mixed = product if mixed is None else mixed + product
                out_ref[row] = (mixed * inverse_refs[group][at]).astype(BF16)

    return pl.pallas_call(
        kernel,
        in_specs=[SMEM_SPEC]
        + [ANY_SPEC] * groups
        + [VMEM_SPEC] * groups
        + part_specs(v_parts),
        out_specs=VMEM_SPEC,
        scratch_shapes=[
            pltpu.VMEM((blocks, BLOCK, HD), BF16),
            pltpu.VMEM((slots, unroll, KMAX // 2, BLOCK, 2 * BLOCK), BF16),
            pltpu.SemaphoreType.DMA((len(v_parts),)),
            pltpu.SemaphoreType.DMA((slots,)),
        ],
        out_shape=jax.ShapeDtypeStruct((rows, BLOCK, HD), BF16),
        compiler_params=pltpu.CompilerParams(vmem_limit_bytes=44 * 2**20),
        cost_estimate=pl.CostEstimate(
            flops=2 * rows * KMAX * BLOCK * BLOCK * HD,
            bytes_accessed=rows * 3 * 2**19,
            transcendentals=0,
        ),
        name="mix",
    )(lists, *[w for w, _ in halves], *[i for _, i in halves], *v_parts)


def after(x, *others):
    return lax.optimization_barrier((x,) + others)[0]


class Ring:
    def __init__(self):
        self.chips = lax.axis_size("narrow") // 2

    def along(self, x, turn):
        steps = [
            (2 * z + core, 2 * ((z + (turn if core == 0 else -turn)) % self.chips) + core)
            for z in range(self.chips)
            for core in range(2)
        ]
        return lax.ppermute(x, "narrow", steps)

    def across(self, x):
        return lax.ppermute(x, "narrow", [(n, n ^ 1) for n in range(2 * self.chips)])


def slots_of(source, part):
    core = part & 1
    apart = (lax.shift_right_logical(source, 1) - lax.shift_right_logical(part, 1)) & 3
    same = (source & 1) == core
    main = jnp.where(core == 0, 3, 1)
    slot_same = jnp.where(apart == 0, 0, jnp.where(apart == 2, 3, jnp.where(apart == main, 1, 2)))
    slot_other = jnp.where(apart == 0, 4, jnp.where(apart == 2, 7, jnp.where(apart == main, 6, 5)))
    return jnp.where(same, slot_same, slot_other)


def shards(query_proj, key_proj, value_proj, positions, key_lists, key_counts):
    frames = lax.axis_size("wide")
    parts = lax.axis_size("narrow")
    part = lax.axis_index("narrow")
    rows = query_proj.shape[0]
    halves = rows // BLOCK
    frame_blocks = parts * halves
    ring = Ring()

    def heads_out(x):
        return lax.all_to_all(x, "wide", split_axis=0, concat_axis=0, tiled=True)

    def blocks_of(x):
        return x.reshape(frames * halves, BLOCK, HD)

    shift = frame_blocks.bit_length() - 1
    frame = lax.shift_right_logical(key_lists, shift)
    inner = key_lists & (frame_blocks - 1)
    source = lax.shift_right_logical(inner, halves.bit_length() - 1)
    places = slots_of(source, part) * (frames * halves) + frame * halves + (inner & (halves - 1))
    mine = lax.dynamic_index_in_dim(
        places.reshape(frames, parts, halves * KMAX), part, 1, keepdims=False
    ).reshape(-1)
    counts = lax.dynamic_index_in_dim(
        key_counts.reshape(frames, parts, halves), part, 1, keepdims=False
    ).reshape(-1)

    k_rot = keys_by_heads(positions, key_proj)
    q_rot, v_heads = others_by_heads(after(positions, k_rot), query_proj, value_proj)

    k_own = after(heads_out(k_rot), v_heads, mine, counts)
    k_main = ring.along(k_own, 1)
    k_opposite = ring.along(k_own, -1)
    k_other = ring.across(k_own)
    v_own = heads_out(after(v_heads, k_own))
    k_far = ring.along(after(k_main, v_own), 1)
    k_main_other = ring.across(k_main)
    k_opposite_other = ring.across(k_opposite)
    q_heads = heads_out(after(q_rot, v_own, k_main_other))
    q = blocks_of(q_heads)
    k_far_other = ring.across(after(k_far, q_heads))
    k_parts = [k_own, k_main, k_opposite, k_far, k_other, k_main_other, k_opposite_other, k_far_other]
    k_parts = [blocks_of(x) for x in k_parts]


    v_ring = after(v_own, k_main_other)
    v_main = ring.along(v_ring, 1)
    v_opposite = ring.along(v_ring, -1)
    v_other = ring.across(v_ring)

    half = frames * halves // 2
    first = weights_of(mine, counts, q, k_parts, 0, half)
    v_main, v_opposite = lax.optimization_barrier((v_main, v_opposite, first[1]))[:2]
    v_far = ring.along(v_main, 1)
    second = weights_of(after(mine, v_main), counts, q, first[2], half, half)
    v_parts = [v_own, v_main, v_opposite, v_far, v_other]
    v_parts += [ring.across(x) for x in (v_main, v_opposite, after(v_far, second[1]))]
    v_parts = [blocks_of(x) for x in v_parts]
    mixed = mix_of(mine, [first[:2], second], v_parts).reshape(frames, rows, HD)
    back = heads_out(mixed)
    return back.transpose(1, 0, 2).reshape(rows, HEADS * HD)


def solution(mesh):
    return jax.shard_map(
        shards,
        mesh=mesh,
        in_specs=(
            P(("wide", "narrow"), None),
            P(("wide", "narrow"), None),
            P(("wide", "narrow"), None),
            P(None, ("wide", "narrow")),
            P(),
            P(),
        ),
        out_specs=P(("wide", "narrow"), None),
        check_vma=False,
    )
```

```python
import functools
import math

import jax
import jax.numpy as jnp
from jax import lax
from jax.experimental import pallas as pl
from jax.experimental.pallas import tpu as pltpu
from jax.sharding import PartitionSpec as P

HEADS = 16
HD = 128
BLOCK = 128
KMAX = 24
MIN_LISTED = 6
PIECES = 4
F32 = jnp.float32
BF16 = jnp.bfloat16
TO_EXP2 = HD**-0.5 * math.log2(math.e)
SECTIONS = ((0, 32), (32, 80), (80, 128))
ROWS_BY_COLS = (((1,), (0,)), ((), ()))
ROWS_BY_ROWS = (((1,), (1,)), ((), ()))


def section_of(lane):
    second = lane >= SECTIONS[1][0]
    third = lane >= SECTIONS[2][0]
    begin = jnp.where(third, SECTIONS[2][0], jnp.where(second, SECTIONS[1][0], 0))
    length = jnp.where(second, SECTIONS[1][1] - SECTIONS[1][0], SECTIONS[0][1])
    number = jnp.where(third, 2, jnp.where(second, 1, 0))
    return begin, length, number


def rotation_of(pos_ref):
    lane = lax.broadcasted_iota(jnp.int32, (3, HD), 1)
    begin, length, number = section_of(lane)
    half = lax.shift_right_logical(length, 1)
    at = lane - begin
    at = jnp.where(at >= half, at - half, at)
    exponent = at.astype(F32) * (-2.0 * math.log(10000.0)) / length.astype(F32)
    mine = number == lax.broadcasted_iota(jnp.int32, (3, HD), 0)
    freqs = jnp.where(mine, jnp.exp(exponent), 0.0)
    angles = lax.dot_general(
        pos_ref[...].astype(F32),
        freqs,
        (((0,), (0,)), ((), ())),
        precision=lax.Precision.HIGHEST,
        preferred_element_type=F32,
    )
    source = lax.broadcasted_iota(jnp.int32, (HD, HD), 0)
    target = lax.broadcasted_iota(jnp.int32, (HD, HD), 1)
    begin, length, number = section_of(target)
    half = lax.shift_right_logical(length, 1)
    lower = target - begin < half
    partner = jnp.where(lower, target + half, target - half)
    sign = jnp.where(lower, -1.0, 1.0)
    pairs = jnp.where(source == partner, sign, 0.0).astype(BF16)
    return jnp.cos(angles), jnp.sin(angles), pairs


def rotate_heads(x_ref, out_ref, cosine, sine, pairs, heads):
    for head in heads:
        x = x_ref[:, head * HD : (head + 1) * HD]
        partner = lax.dot_general(x, pairs, ROWS_BY_COLS, preferred_element_type=F32)
        out_ref[head] = (x.astype(F32) * cosine + partner * sine).astype(BF16)


def keys_kernel(pos_hbm, k_hbm, out_ref, pos_ref, k_ref, sems):
    positions = pltpu.make_async_copy(pos_hbm, pos_ref, sems.at[PIECES])
    positions.start()
    width = HEADS // PIECES * HD
    pieces = [
        pltpu.make_async_copy(
            k_hbm.at[:, pl.ds(n * width, width)], k_ref.at[:, pl.ds(n * width, width)], sems.at[n]
        )
        for n in range(PIECES)
    ]
    for piece in pieces:
        piece.start()
    positions.wait()
    rotation = rotation_of(pos_ref)
    for n, piece in enumerate(pieces):
        piece.wait()
        heads = range(n * HEADS // PIECES, (n + 1) * HEADS // PIECES)
        rotate_heads(k_ref, out_ref, *rotation, heads)


def others_kernel(pos_ref, q_ref, v_ref, q_out, v_out):
    for head in range(HEADS):
        v_out[head] = v_ref[:, head * HD : (head + 1) * HD]
    rotate_heads(q_ref, q_out, *rotation_of(pos_ref), range(HEADS))


def keys_by_heads(positions, x):
    rows = x.shape[0]
    hbm = pl.BlockSpec(memory_space=pltpu.HBM)
    return pl.pallas_call(
        keys_kernel,
        in_specs=[hbm, hbm],
        out_shape=jax.ShapeDtypeStruct((HEADS, rows, HD), BF16),
        scratch_shapes=[
            pltpu.VMEM(positions.shape, jnp.int32),
            pltpu.VMEM(x.shape, BF16),
            pltpu.SemaphoreType.DMA((PIECES + 1,)),
        ],
        compiler_params=pltpu.CompilerParams(vmem_limit_bytes=60 * 2**20),
        name="rotate_keys",
    )(positions, x)


def others_by_heads(positions, q, v):
    heads = jax.ShapeDtypeStruct((HEADS, q.shape[0], HD), BF16)
    return pl.pallas_call(
        others_kernel,
        out_shape=[heads, heads],
        compiler_params=pltpu.CompilerParams(vmem_limit_bytes=50 * 2**20),
        name="rotate_queries",
    )(positions, q, v)


def load_blocks(sources, target, sems, then=()):
    copies = []
    at = 0
    for n, source in enumerate(sources):
        blocks = source.shape[0]
        copies.append(pltpu.make_async_copy(source, target.at[pl.ds(at, blocks)], sems.at[n]))
        at += blocks
    for copy in copies:
        copy.start()
    for copy in then:
        copy.start()
    for copy in copies:
        copy.wait()


def listed_pair(ref, lists_ref, row, pair):
    at = row * KMAX + 2 * pair
    return jnp.concatenate([ref[lists_ref[at]], ref[lists_ref[at + 1]]], axis=0)


def weights_kernel(sources, unroll, first, rows, lists_ref, counts_ref, q_ref, *refs):
    if sources:
        k_parts = refs[:sources]
        weights_out, inverse_ref, k_ref, s_ref, w_ref, out_sems, sems = refs[sources:]
        load_blocks(k_parts, k_ref, sems)
    else:
        k_ref, weights_out, inverse_ref, s_ref, w_ref, out_sems = refs
    turns = rows // unroll

    def leave(turn, slot):
        return pltpu.make_async_copy(
            w_ref.at[slot], weights_out.at[pl.ds(turn * unroll, unroll)], out_sems.at[slot]
        )

    def row_weights(row, slot, n):
        query = q_ref[first + row]
        largest = None
        for pair in range(KMAX // 2):
            scores = lax.dot_general(
                query,
                listed_pair(k_ref, lists_ref, first + row, pair),
                ROWS_BY_ROWS,
                preferred_element_type=F32,
            )
            s_ref[n, pair] = scores
            for half in range(2):
                part = scores[:, half * BLOCK : (half + 1) * BLOCK]
                largest = part if largest is None else jnp.maximum(largest, part)
        shift = jnp.broadcast_to(
            jnp.max(largest, axis=1, keepdims=True) * TO_EXP2, (BLOCK, BLOCK)
        )
        count = counts_ref[first + row]
        total = None
        for entry in range(KMAX):
            pair, half = divmod(entry, 2)
            shift_here = shift
            if entry >= MIN_LISTED:
                shift_here = shift + jnp.where(entry < count, 0.0, 1e30)
            lanes = slice(half * BLOCK, (half + 1) * BLOCK)
            part = jnp.exp2(s_ref[n, pair, :, lanes] * TO_EXP2 - shift_here)
            total = part if total is None else total + part
            w_ref[slot, n, pair, :, lanes] = part.astype(BF16)
        inverse_ref[row] = jnp.broadcast_to(
            1.0 / jnp.sum(total, axis=1, keepdims=True), (BLOCK, BLOCK)
        )

    def step(turn, carry):
        slot = turn & 1

        @pl.when(turn >= 2)
        def _():
            leave(turn - 2, slot).wait()

        for n in range(unroll):
            row_weights(turn * unroll + n, slot, n)
        leave(turn, slot).start()
        return carry

    lax.fori_loop(0, turns, step, 0)
    for turn in range(max(turns - 2, 0), turns):
        leave(turn, turn & 1).wait()


SMEM_SPEC = pl.BlockSpec(memory_space=pltpu.SMEM)
VMEM_SPEC = pl.BlockSpec(memory_space=pltpu.VMEM)
ANY_SPEC = pl.BlockSpec(memory_space=pl.ANY)


def part_specs(parts):
    half = len(parts) // 2
    return ([ANY_SPEC] * (half - 1) + [VMEM_SPEC]) * 2


def weights_of(lists, counts, q, k_parts, first, rows, unroll=4):
    whole = not isinstance(k_parts, list)
    parts = [k_parts] if whole else k_parts
    sources = 0 if whole else len(parts)
    blocks = sum(part.shape[0] for part in parts)
    group = (unroll, KMAX // 2, BLOCK, 2 * BLOCK)
    out_shape = [
        pltpu.HBM((rows,) + group[1:], BF16),
        jax.ShapeDtypeStruct((rows, BLOCK, BLOCK), F32),
    ]
    scratch = [
        pltpu.VMEM(group, F32),
        pltpu.VMEM((2,) + group, BF16),
        pltpu.SemaphoreType.DMA((2,)),
    ]
    out_specs = [pl.BlockSpec(memory_space=pltpu.HBM), VMEM_SPEC]
    if not whole:
        out_shape.append(pltpu.VMEM((blocks, BLOCK, HD), BF16))
        out_specs.append(VMEM_SPEC)
        scratch.append(pltpu.SemaphoreType.DMA((sources,)))
    return pl.pallas_call(
        functools.partial(weights_kernel, sources, unroll, first, rows),
        in_specs=[SMEM_SPEC, SMEM_SPEC, VMEM_SPEC] + ([VMEM_SPEC] if whole else part_specs(parts)),
        out_specs=out_specs,
        scratch_shapes=scratch,
        out_shape=out_shape,
        compiler_params=pltpu.CompilerParams(vmem_limit_bytes=20 * 2**20),
        cost_estimate=pl.CostEstimate(
            flops=2 * rows * KMAX * BLOCK * BLOCK * HD,
            bytes_accessed=rows * 3 * 2**20,
            transcendentals=rows * KMAX * BLOCK * BLOCK,
        ),
        name="weights",
    )(lists, counts, q, *parts)


def near_values(v_parts):
    blocks = sum(part.shape[0] for part in v_parts)
    size = v_parts[0].shape[0]
    far = len(v_parts) // 2 - 1
    near = [n for n in range(len(v_parts)) if n % (far + 1) != far]

    def kernel(*refs):
        parts, whole, sems = refs[: len(near)], refs[-2], refs[-1]
        copies = [
            pltpu.make_async_copy(part, whole.at[pl.ds(n * size, size)], sems.at[at])
            for at, (n, part) in enumerate(zip(near, parts))
        ]
        for copy in copies:
            copy.start()
        for copy in copies:
            copy.wait()

    return pl.pallas_call(
        kernel,
        in_specs=[ANY_SPEC] * len(near),
        out_specs=VMEM_SPEC,
        scratch_shapes=[pltpu.SemaphoreType.DMA((len(near),))],
        out_shape=pltpu.VMEM((blocks, BLOCK, HD), BF16),
        compiler_params=pltpu.CompilerParams(vmem_limit_bytes=10 * 2**20),
        cost_estimate=pl.CostEstimate(flops=0, bytes_accessed=12 * 2**20, transcendentals=0),
        name="near_values",
    )(*[v_parts[n] for n in near])


def mix_of(lists, halves, v_near, v_parts, unroll=4, slots=4):
    groups = len(halves)
    group_rows = halves[0][0].shape[0]
    rows = groups * group_rows
    turns = rows // unroll
    size = v_parts[0].shape[0]
    places = [len(v_parts) * 2 - 1, len(v_parts) * 4 - 1]

    def kernel(lists_ref, *refs):
        weights_refs = refs[:groups]
        inverse_refs = refs[groups : 2 * groups]
        v_refs = refs[2 * groups + 1 : 2 * groups + 1 + len(v_parts)]
        out_ref, v_ref, w_ref, sems, w_sems = refs[2 * groups + 1 + len(v_parts) :]

        def fetch(turn):
            group, at = divmod(turn * unroll, group_rows)
            slot = turn % slots
            return pltpu.make_async_copy(
                weights_refs[group].at[pl.ds(at, unroll)], w_ref.at[slot], w_sems.at[slot]
            )

        fetch(0).start()
        copies = [
            pltpu.make_async_copy(part, v_ref.at[pl.ds(n * size, size)], sems.at[at])
            for at, (n, part) in enumerate(zip(places, v_refs))
        ]
        for copy in copies + [fetch(n) for n in range(1, slots - 1)]:
            copy.start()
        for copy in copies:
            copy.wait()
        for turn in range(turns):
            fetch(turn).wait()
            if turn + slots - 1 < turns:
                fetch(turn + slots - 1).start()
            for n in range(unroll):
                row = turn * unroll + n
                group, at = divmod(row, group_rows)
                mixed = None
                for pair in range(KMAX // 2):
                    product = lax.dot_general(
                        w_ref[turn % slots, n, pair],
                        listed_pair(v_ref, lists_ref, row, pair),
                        ROWS_BY_COLS,
                        preferred_element_type=F32,
                    )
                    mixed = product if mixed is None else mixed + product
                out_ref[row] = (mixed * inverse_refs[group][at]).astype(BF16)

    return pl.pallas_call(
        kernel,
        in_specs=[SMEM_SPEC]
        + [ANY_SPEC] * groups
        + [VMEM_SPEC] * groups
        + [VMEM_SPEC] * (1 + len(v_parts)),
        out_specs=[VMEM_SPEC, VMEM_SPEC],
        input_output_aliases={1 + 2 * groups: 1},
        scratch_shapes=[
            pltpu.VMEM((slots, unroll, KMAX // 2, BLOCK, 2 * BLOCK), BF16),
            pltpu.SemaphoreType.DMA((len(v_parts),)),
            pltpu.SemaphoreType.DMA((slots,)),
        ],
        out_shape=[jax.ShapeDtypeStruct((rows, BLOCK, HD), BF16), pltpu.VMEM(v_near.shape, BF16)],
        compiler_params=pltpu.CompilerParams(vmem_limit_bytes=26 * 2**20),
        cost_estimate=pl.CostEstimate(
            flops=2 * rows * KMAX * BLOCK * BLOCK * HD,
            bytes_accessed=rows * 3 * 2**19,
            transcendentals=0,
        ),
        name="mix",
    )(lists, *[w for w, _ in halves], *[i for _, i in halves], v_near, *v_parts)[0]


def after(x, *others):
    return lax.optimization_barrier((x,) + others)[0]


class Ring:
    def __init__(self):
        self.chips = lax.axis_size("narrow") // 2

    def along(self, x, turn):
        steps = [
            (2 * z + core, 2 * ((z + (turn if core == 0 else -turn)) % self.chips) + core)
            for z in range(self.chips)
            for core in range(2)
        ]
        return lax.ppermute(x, "narrow", steps)

    def across(self, x):
        return lax.ppermute(x, "narrow", [(n, n ^ 1) for n in range(2 * self.chips)])


def slots_of(source, part):
    core = part & 1
    apart = (lax.shift_right_logical(source, 1) - lax.shift_right_logical(part, 1)) & 3
    same = (source & 1) == core
    main = jnp.where(core == 0, 3, 1)
    slot_same = jnp.where(apart == 0, 0, jnp.where(apart == 2, 3, jnp.where(apart == main, 1, 2)))
    slot_other = jnp.where(apart == 0, 4, jnp.where(apart == 2, 7, jnp.where(apart == main, 6, 5)))
    return jnp.where(same, slot_same, slot_other)


def shards(query_proj, key_proj, value_proj, positions, key_lists, key_counts):
    frames = lax.axis_size("wide")
    parts = lax.axis_size("narrow")
    part = lax.axis_index("narrow")
    rows = query_proj.shape[0]
    halves = rows // BLOCK
    frame_blocks = parts * halves
    ring = Ring()

    def heads_out(x):
        return lax.all_to_all(x, "wide", split_axis=0, concat_axis=0, tiled=True)

    def blocks_of(x):
        return x.reshape(frames * halves, BLOCK, HD)

    shift = frame_blocks.bit_length() - 1
    frame = lax.shift_right_logical(key_lists, shift)
    inner = key_lists & (frame_blocks - 1)
    source = lax.shift_right_logical(inner, halves.bit_length() - 1)
    places = slots_of(source, part) * (frames * halves) + frame * halves + (inner & (halves - 1))
    mine = lax.dynamic_index_in_dim(
        places.reshape(frames, parts, halves * KMAX), part, 1, keepdims=False
    ).reshape(-1)
    counts = lax.dynamic_index_in_dim(
        key_counts.reshape(frames, parts, halves), part, 1, keepdims=False
    ).reshape(-1)

    k_rot = keys_by_heads(positions, key_proj)
    q_rot, v_heads = others_by_heads(after(positions, k_rot), query_proj, value_proj)

    k_own = after(heads_out(k_rot), v_heads, mine, counts)
    k_main = ring.along(k_own, 1)
    k_opposite = ring.along(k_own, -1)
    k_other = ring.across(k_own)
    v_own = heads_out(after(v_heads, k_own))
    k_far = ring.along(after(k_main, v_own), 1)
    k_main_other = ring.across(k_main)
    k_opposite_other = ring.across(k_opposite)
    q_heads = heads_out(after(q_rot, v_own, k_main_other))
    q = blocks_of(q_heads)
    k_far_other = ring.across(after(k_far, q_heads))
    k_parts = [k_own, k_main, k_opposite, k_far, k_other, k_main_other, k_opposite_other, k_far_other]
    k_parts = [blocks_of(x) for x in k_parts]


    v_ring = after(v_own, k_main_other)
    v_main = ring.along(v_ring, 1)
    v_opposite = ring.along(v_ring, -1)
    v_other = ring.across(v_ring)

    half = frames * halves // 2
    first = weights_of(mine, counts, q, k_parts, 0, half)
    v_main, v_opposite = lax.optimization_barrier((v_main, v_opposite, first[1]))[:2]
    v_far = ring.along(v_main, 1)
    second = weights_of(after(mine, v_main), counts, q, first[2], half, half)
    v_parts = [v_own, v_main, v_opposite, v_far, v_other]
    v_parts += [ring.across(x) for x in (v_main, v_opposite, after(v_far, second[1]))]
    v_parts = [blocks_of(x) for x in v_parts]
    v_near = near_values([after(v_parts[0], second[1])] + v_parts[1:])
    mixed = mix_of(mine, [first[:2], second], v_near, [v_parts[3], v_parts[7]])
    mixed = mixed.reshape(frames, rows, HD)
    back = heads_out(mixed)
    return back.transpose(1, 0, 2).reshape(rows, HEADS * HD)


def solution(mesh):
    return jax.shard_map(
        shards,
        mesh=mesh,
        in_specs=(
            P(("wide", "narrow"), None),
            P(("wide", "narrow"), None),
            P(("wide", "narrow"), None),
            P(None, ("wide", "narrow")),
            P(),
            P(),
        ),
        out_specs=P(("wide", "narrow"), None),
        check_vma=False,
    )
```

```python
import functools
import math

import jax
import jax.numpy as jnp
from jax import lax
from jax.experimental import pallas as pl
from jax.experimental.pallas import tpu as pltpu
from jax.sharding import PartitionSpec as P

HEADS = 16
HD = 128
BLOCK = 128
KMAX = 24
MIN_LISTED = 6
PIECES = 4
F32 = jnp.float32
BF16 = jnp.bfloat16
TO_EXP2 = HD**-0.5 * math.log2(math.e)
SECTIONS = ((0, 32), (32, 80), (80, 128))
ROWS_BY_COLS = (((1,), (0,)), ((), ()))
ROWS_BY_ROWS = (((1,), (1,)), ((), ()))


def section_of(lane):
    second = lane >= SECTIONS[1][0]
    third = lane >= SECTIONS[2][0]
    begin = jnp.where(third, SECTIONS[2][0], jnp.where(second, SECTIONS[1][0], 0))
    length = jnp.where(second, SECTIONS[1][1] - SECTIONS[1][0], SECTIONS[0][1])
    number = jnp.where(third, 2, jnp.where(second, 1, 0))
    return begin, length, number


def rotation_of(pos_ref):
    lane = lax.broadcasted_iota(jnp.int32, (3, HD), 1)
    begin, length, number = section_of(lane)
    half = lax.shift_right_logical(length, 1)
    at = lane - begin
    at = jnp.where(at >= half, at - half, at)
    exponent = at.astype(F32) * (-2.0 * math.log(10000.0)) / length.astype(F32)
    mine = number == lax.broadcasted_iota(jnp.int32, (3, HD), 0)
    freqs = jnp.where(mine, jnp.exp(exponent), 0.0)
    angles = lax.dot_general(
        pos_ref[...].astype(F32),
        freqs,
        (((0,), (0,)), ((), ())),
        precision=lax.Precision.HIGHEST,
        preferred_element_type=F32,
    )
    source = lax.broadcasted_iota(jnp.int32, (HD, HD), 0)
    target = lax.broadcasted_iota(jnp.int32, (HD, HD), 1)
    begin, length, number = section_of(target)
    half = lax.shift_right_logical(length, 1)
    lower = target - begin < half
    partner = jnp.where(lower, target + half, target - half)
    sign = jnp.where(lower, -1.0, 1.0)
    pairs = jnp.where(source == partner, sign, 0.0).astype(BF16)
    return jnp.cos(angles), jnp.sin(angles), pairs


def rotate_heads(x_ref, out_ref, cosine, sine, pairs, heads):
    for head in heads:
        x = x_ref[:, head * HD : (head + 1) * HD]
        partner = lax.dot_general(x, pairs, ROWS_BY_COLS, preferred_element_type=F32)
        out_ref[head] = (x.astype(F32) * cosine + partner * sine).astype(BF16)


def keys_kernel(pos_hbm, k_hbm, out_ref, pos_ref, k_ref, sems):
    positions = pltpu.make_async_copy(pos_hbm, pos_ref, sems.at[PIECES])
    positions.start()
    width = HEADS // PIECES * HD
    pieces = [
        pltpu.make_async_copy(
            k_hbm.at[:, pl.ds(n * width, width)], k_ref.at[:, pl.ds(n * width, width)], sems.at[n]
        )
        for n in range(PIECES)
    ]
    for piece in pieces:
        piece.start()
    positions.wait()
    rotation = rotation_of(pos_ref)
    for n, piece in enumerate(pieces):
        piece.wait()
        heads = range(n * HEADS // PIECES, (n + 1) * HEADS // PIECES)
        rotate_heads(k_ref, out_ref, *rotation, heads)


def others_kernel(pos_ref, q_ref, v_ref, q_out, v_out):
    for head in range(HEADS):
        v_out[head] = v_ref[:, head * HD : (head + 1) * HD]
    rotate_heads(q_ref, q_out, *rotation_of(pos_ref), range(HEADS))


def keys_by_heads(positions, x):
    rows = x.shape[0]
    hbm = pl.BlockSpec(memory_space=pltpu.HBM)
    return pl.pallas_call(
        keys_kernel,
        in_specs=[hbm, hbm],
        out_shape=jax.ShapeDtypeStruct((HEADS, rows, HD), BF16),
        scratch_shapes=[
            pltpu.VMEM(positions.shape, jnp.int32),
            pltpu.VMEM(x.shape, BF16),
            pltpu.SemaphoreType.DMA((PIECES + 1,)),
        ],
        compiler_params=pltpu.CompilerParams(vmem_limit_bytes=60 * 2**20),
        name="rotate_keys",
    )(positions, x)


def others_by_heads(positions, q, v):
    heads = jax.ShapeDtypeStruct((HEADS, q.shape[0], HD), BF16)
    return pl.pallas_call(
        others_kernel,
        out_shape=[heads, heads],
        compiler_params=pltpu.CompilerParams(vmem_limit_bytes=50 * 2**20),
        name="rotate_queries",
    )(positions, q, v)


def load_blocks(sources, target, sems, then=()):
    copies = []
    at = 0
    for n, source in enumerate(sources):
        blocks = source.shape[0]
        copies.append(pltpu.make_async_copy(source, target.at[pl.ds(at, blocks)], sems.at[n]))
        at += blocks
    for copy in copies:
        copy.start()
    for copy in then:
        copy.start()
    for copy in copies:
        copy.wait()


def listed_pair(ref, lists_ref, row, pair):
    at = row * KMAX + 2 * pair
    return jnp.concatenate([ref[lists_ref[at]], ref[lists_ref[at + 1]]], axis=0)


def weights_kernel(sources, unroll, first, rows, lists_ref, counts_ref, q_ref, *refs):
    if sources:
        k_parts = refs[:sources]
        weights_out, inverse_ref, k_ref, s_ref, w_ref, out_sems, sems = refs[sources:]
        load_blocks(k_parts, k_ref, sems)
    else:
        k_ref, weights_out, inverse_ref, s_ref, w_ref, out_sems = refs
    turns = rows // unroll

    def leave(turn, slot):
        return pltpu.make_async_copy(
            w_ref.at[slot], weights_out.at[pl.ds(turn * unroll, unroll)], out_sems.at[slot]
        )

    def row_weights(row, slot, n):
        query = q_ref[first + row]
        largest = None
        for pair in range(KMAX // 2):
            scores = lax.dot_general(
                query,
                listed_pair(k_ref, lists_ref, first + row, pair),
                ROWS_BY_ROWS,
                preferred_element_type=F32,
            )
            s_ref[n, pair] = scores
            for half in range(2):
                part = scores[:, half * BLOCK : (half + 1) * BLOCK]
                largest = part if largest is None else jnp.maximum(largest, part)
        shift = jnp.broadcast_to(
            jnp.max(largest, axis=1, keepdims=True) * TO_EXP2, (BLOCK, BLOCK)
        )
        count = counts_ref[first + row]
        total = None
        for entry in range(KMAX):
            pair, half = divmod(entry, 2)
            shift_here = shift
            if entry >= MIN_LISTED:
                shift_here = shift + jnp.where(entry < count, 0.0, 1e30)
            lanes = slice(half * BLOCK, (half + 1) * BLOCK)
            part = jnp.exp2(s_ref[n, pair, :, lanes] * TO_EXP2 - shift_here)
            total = part if total is None else total + part
            w_ref[slot, n, pair, :, lanes] = part.astype(BF16)
        inverse_ref[row] = jnp.broadcast_to(
            1.0 / jnp.sum(total, axis=1, keepdims=True), (BLOCK, BLOCK)
        )

    def step(turn, carry):
        slot = turn & 1

        @pl.when(turn >= 2)
        def _():
            leave(turn - 2, slot).wait()

        for n in range(unroll):
            row_weights(turn * unroll + n, slot, n)
        leave(turn, slot).start()
        return carry

    lax.fori_loop(0, turns, step, 0)
    for turn in range(max(turns - 2, 0), turns):
        leave(turn, turn & 1).wait()


SMEM_SPEC = pl.BlockSpec(memory_space=pltpu.SMEM)
VMEM_SPEC = pl.BlockSpec(memory_space=pltpu.VMEM)
ANY_SPEC = pl.BlockSpec(memory_space=pl.ANY)


def part_specs(parts):
    half = len(parts) // 2
    return ([ANY_SPEC] * (half - 1) + [VMEM_SPEC]) * 2


def weights_of(lists, counts, q, k_parts, first, rows, unroll=4):
    whole = not isinstance(k_parts, list)
    parts = [k_parts] if whole else k_parts
    sources = 0 if whole else len(parts)
    blocks = sum(part.shape[0] for part in parts)
    group = (unroll, KMAX // 2, BLOCK, 2 * BLOCK)
    out_shape = [
        pltpu.HBM((rows,) + group[1:], BF16),
        jax.ShapeDtypeStruct((rows, BLOCK, BLOCK), F32),
    ]
    scratch = [
        pltpu.VMEM(group, F32),
        pltpu.VMEM((2,) + group, BF16),
        pltpu.SemaphoreType.DMA((2,)),
    ]
    out_specs = [pl.BlockSpec(memory_space=pltpu.HBM), VMEM_SPEC]
    if not whole:
        out_shape.append(pltpu.VMEM((blocks, BLOCK, HD), BF16))
        out_specs.append(VMEM_SPEC)
        scratch.append(pltpu.SemaphoreType.DMA((sources,)))
    return pl.pallas_call(
        functools.partial(weights_kernel, sources, unroll, first, rows),
        in_specs=[SMEM_SPEC, SMEM_SPEC, VMEM_SPEC] + ([VMEM_SPEC] if whole else part_specs(parts)),
        out_specs=out_specs,
        scratch_shapes=scratch,
        out_shape=out_shape,
        compiler_params=pltpu.CompilerParams(vmem_limit_bytes=20 * 2**20),
        cost_estimate=pl.CostEstimate(
            flops=2 * rows * KMAX * BLOCK * BLOCK * HD,
            bytes_accessed=rows * 3 * 2**20,
            transcendentals=rows * KMAX * BLOCK * BLOCK,
        ),
        name="weights",
    )(lists, counts, q, *parts)


def near_values(v_parts):
    blocks = sum(part.shape[0] for part in v_parts)
    size = v_parts[0].shape[0]
    far = len(v_parts) // 2 - 1
    near = [n for n in range(len(v_parts)) if n % (far + 1) != far]

    def kernel(*refs):
        parts, whole, sems = refs[: len(near)], refs[-2], refs[-1]
        copies = [
            pltpu.make_async_copy(part, whole.at[pl.ds(n * size, size)], sems.at[at])
            for at, (n, part) in enumerate(zip(near, parts))
        ]
        for copy in copies:
            copy.start()
        for copy in copies:
            copy.wait()

    return pl.pallas_call(
        kernel,
        in_specs=[ANY_SPEC] * len(near),
        out_specs=VMEM_SPEC,
        scratch_shapes=[pltpu.SemaphoreType.DMA((len(near),))],
        out_shape=pltpu.VMEM((blocks, BLOCK, HD), BF16),
        compiler_params=pltpu.CompilerParams(vmem_limit_bytes=10 * 2**20),
        cost_estimate=pl.CostEstimate(flops=0, bytes_accessed=12 * 2**20, transcendentals=0),
        name="near_values",
    )(*[v_parts[n] for n in near])


def mix_of(lists, halves, v_near, v_parts, unroll=4, slots=4):
    groups = len(halves)
    rows = sum(weights.shape[0] for weights, _ in halves)
    places_of = [(n, at) for n in range(groups) for at in range(halves[n][0].shape[0])]
    turns = rows // unroll
    size = v_parts[0].shape[0]
    places = [len(v_parts) * 2 - 1, len(v_parts) * 4 - 1]

    def kernel(lists_ref, *refs):
        weights_refs = refs[:groups]
        inverse_refs = refs[groups : 2 * groups]
        v_refs = refs[2 * groups + 1 : 2 * groups + 1 + len(v_parts)]
        out_ref, v_ref, w_ref, sems, w_sems = refs[2 * groups + 1 + len(v_parts) :]

        def fetch(turn):
            group, at = places_of[turn * unroll]
            slot = turn % slots
            return pltpu.make_async_copy(
                weights_refs[group].at[pl.ds(at, unroll)], w_ref.at[slot], w_sems.at[slot]
            )

        fetch(0).start()
        copies = [
            pltpu.make_async_copy(part, v_ref.at[pl.ds(n * size, size)], sems.at[at])
            for at, (n, part) in enumerate(zip(places, v_refs))
        ]
        for copy in copies + [fetch(n) for n in range(1, slots - 1)]:
            copy.start()
        for copy in copies:
            copy.wait()
        for turn in range(turns):
            fetch(turn).wait()
            if turn + slots - 1 < turns:
                fetch(turn + slots - 1).start()
            for n in range(unroll):
                row = turn * unroll + n
                group, at = places_of[row]
                mixed = None
                for pair in range(KMAX // 2):
                    product = lax.dot_general(
                        w_ref[turn % slots, n, pair],
                        listed_pair(v_ref, lists_ref, row, pair),
                        ROWS_BY_COLS,
                        preferred_element_type=F32,
                    )
                    mixed = product if mixed is None else mixed + product
                out_ref[row] = (mixed * inverse_refs[group][at]).astype(BF16)

    return pl.pallas_call(
        kernel,
        in_specs=[SMEM_SPEC]
        + [ANY_SPEC] * groups
        + [VMEM_SPEC] * groups
        + [VMEM_SPEC] * (1 + len(v_parts)),
        out_specs=[VMEM_SPEC, VMEM_SPEC],
        input_output_aliases={1 + 2 * groups: 1},
        scratch_shapes=[
            pltpu.VMEM((slots, unroll, KMAX // 2, BLOCK, 2 * BLOCK), BF16),
            pltpu.SemaphoreType.DMA((len(v_parts),)),
            pltpu.SemaphoreType.DMA((slots,)),
        ],
        out_shape=[jax.ShapeDtypeStruct((rows, BLOCK, HD), BF16), pltpu.VMEM(v_near.shape, BF16)],
        compiler_params=pltpu.CompilerParams(vmem_limit_bytes=26 * 2**20),
        cost_estimate=pl.CostEstimate(
            flops=2 * rows * KMAX * BLOCK * BLOCK * HD,
            bytes_accessed=rows * 3 * 2**19,
            transcendentals=0,
        ),
        name="mix",
    )(lists, *[w for w, _ in halves], *[i for _, i in halves], v_near, *v_parts)[0]


def after(x, *others):
    return lax.optimization_barrier((x,) + others)[0]


class Ring:
    def __init__(self):
        self.chips = lax.axis_size("narrow") // 2

    def along(self, x, turn):
        steps = [
            (2 * z + core, 2 * ((z + (turn if core == 0 else -turn)) % self.chips) + core)
            for z in range(self.chips)
            for core in range(2)
        ]
        return lax.ppermute(x, "narrow", steps)

    def across(self, x):
        return lax.ppermute(x, "narrow", [(n, n ^ 1) for n in range(2 * self.chips)])


def slots_of(source, part):
    core = part & 1
    apart = (lax.shift_right_logical(source, 1) - lax.shift_right_logical(part, 1)) & 3
    same = (source & 1) == core
    main = jnp.where(core == 0, 3, 1)
    slot_same = jnp.where(apart == 0, 0, jnp.where(apart == 2, 3, jnp.where(apart == main, 1, 2)))
    slot_other = jnp.where(apart == 0, 4, jnp.where(apart == 2, 7, jnp.where(apart == main, 6, 5)))
    return jnp.where(same, slot_same, slot_other)


def shards(query_proj, key_proj, value_proj, positions, key_lists, key_counts):
    frames = lax.axis_size("wide")
    parts = lax.axis_size("narrow")
    part = lax.axis_index("narrow")
    rows = query_proj.shape[0]
    halves = rows // BLOCK
    frame_blocks = parts * halves
    ring = Ring()

    def heads_out(x):
        return lax.all_to_all(x, "wide", split_axis=0, concat_axis=0, tiled=True)

    def blocks_of(x):
        return x.reshape(frames * halves, BLOCK, HD)

    shift = frame_blocks.bit_length() - 1
    frame = lax.shift_right_logical(key_lists, shift)
    inner = key_lists & (frame_blocks - 1)
    source = lax.shift_right_logical(inner, halves.bit_length() - 1)
    places = slots_of(source, part) * (frames * halves) + frame * halves + (inner & (halves - 1))
    mine = lax.dynamic_index_in_dim(
        places.reshape(frames, parts, halves * KMAX), part, 1, keepdims=False
    ).reshape(-1)
    counts = lax.dynamic_index_in_dim(
        key_counts.reshape(frames, parts, halves), part, 1, keepdims=False
    ).reshape(-1)

    k_rot = keys_by_heads(positions, key_proj)
    q_rot, v_heads = others_by_heads(after(positions, k_rot), query_proj, value_proj)

    k_own = after(heads_out(k_rot), v_heads, mine, counts)
    k_main = ring.along(k_own, 1)
    k_opposite = ring.along(k_own, -1)
    k_other = ring.across(k_own)
    v_own = heads_out(after(v_heads, k_own))
    k_far = ring.along(after(k_main, v_own), 1)
    k_main_other = ring.across(k_main)
    k_opposite_other = ring.across(k_opposite)
    q_heads = heads_out(after(q_rot, v_own, k_main_other))
    q = blocks_of(q_heads)
    k_far_other = ring.across(after(k_far, q_heads))
    k_parts = [k_own, k_main, k_opposite, k_far, k_other, k_main_other, k_opposite_other, k_far_other]
    k_parts = [blocks_of(x) for x in k_parts]


    v_ring = after(v_own, k_main_other)
    v_main = ring.along(v_ring, 1)
    v_opposite = ring.along(v_ring, -1)
    v_other = ring.across(v_ring)

    early = frames * halves * 5 // 8
    late = frames * halves - early
    first = weights_of(mine, counts, q, k_parts, 0, early)
    v_main = after(v_main, first[1])
    v_far = ring.along(v_main, 1)
    second = weights_of(after(mine, v_main), counts, q, first[2], early, late)
    v_parts = [v_own, v_main, v_opposite, v_far, v_other]
    v_parts += [ring.across(x) for x in (v_main, v_opposite, after(v_far, second[1]))]
    v_parts = [blocks_of(x) for x in v_parts]
    v_near = near_values([after(v_parts[0], second[1])] + v_parts[1:])
    mixed = mix_of(mine, [first[:2], second], v_near, [v_parts[3], v_parts[7]])
    mixed = mixed.reshape(frames, rows, HD)
    back = heads_out(mixed)
    return back.transpose(1, 0, 2).reshape(rows, HEADS * HD)


def solution(mesh):
    return jax.shard_map(
        shards,
        mesh=mesh,
        in_specs=(
            P(("wide", "narrow"), None),
            P(("wide", "narrow"), None),
            P(("wide", "narrow"), None),
            P(None, ("wide", "narrow")),
            P(),
            P(),
        ),
        out_specs=P(("wide", "narrow"), None),
        check_vma=False,
    )
```
